32 devices in a mesh: groups: 2 (over y), band: 16 (over z, x, core).
Axes of the slice: x: 2, y: 2, z: 4, core: 2. Of those that a mesh axis runs over, the one named last changes fastest.
Arguments:
- grid_feats: bfloat16 [8192, 227], P(('groups', 'band')), parts along dimension 0, may hold values from -6 to 6
- mesh_feat: bfloat16 [4096, 512], P('band'), may hold values from -6 to 6
- edge_latent: bfloat16 [32768, 512], P('band'), may hold values from -6 to 6
- g2m_owner: int32 [4096, 1], P('band'), may hold values from 0 to 15; in each aligned block of 256 rows (0 to 255, 256 to 511, ...) at most 32 rows name the same one
- g2m_node: int32 [4096], P('band'), may hold values from 0 to 255
- edge_sender: int32 [32768], P('band'), may hold values from 0 to 319
- edge_receiver: int32 [32768], P('band'), may hold values from 0 to 255
- border_low: int32 [16, 32], P('band'), may hold values from 0 to 255
- border_high: int32 [16, 32], P('band'), may hold values from 0 to 255
- w_embed: bfloat16 [227, 512], replicated, may hold values from -0.375 to 0.375
- w_g2m: bfloat16 [512, 512], replicated, may hold values from -0.25 to 0.25
- gain_enc: float32 [512], replicated, may hold values from 0.1 to 1.9
- w_edge_in: bfloat16 [2, 1536, 512], replicated, may hold values from -0.15625 to 0.15625
- w_edge_out: bfloat16 [2, 512, 512], replicated, may hold values from -0.25 to 0.25
- gain_edge: float32 [2, 512], replicated, may hold values from 0.1 to 1.9
- w_node_in: bfloat16 [2, 1024, 512], replicated, may hold values from -0.1875 to 0.1875
- w_node_out: bfloat16 [2, 512, 512], replicated, may hold values from -0.25 to 0.25
- gain_node: float32 [2, 512], replicated, may hold values from 0.1 to 1.9
- w_m2g_mesh: bfloat16 [512, 512], replicated, may hold values from -0.25 to 0.25
- w_m2g_grid: bfloat16 [512, 512], replicated, may hold values from -0.25 to 0.25
- w_out: bfloat16 [512, 227], replicated, may hold values from -0.25 to 0.25
Outputs:
- prediction: bfloat16 [8192, 227], P(('groups', 'band')), parts along dimension 0
The draws below stay inside these ranges and needn't reach their ends.
There are 2 independent parts, one for each index of `groups`. The reference program is written for one: setup_inputs(seed, part) draws one part's arguments, and reference() takes and returns one part's arrays. A program takes and returns all parts, laid end to end along the dimension named above; an argument that names none is the same for every part. Nothing has to cross between parts.
Inputs may be any that keep to these rules, and one draw needn't show every extreme that they name: `g2m_owner`: among the grid points of one partition at most 32 name the same owner, and in some partition one owner is named by exactly 32 of them. `edge_sender`: values below 256 name the partition's own nodes, the next 32 values the previous partition's high border list, the last 32 the next partition's low border list.
All inputs are finite; a program needn't handle non-finite values.
Results may differ from the reference program's by a relative error of at most 0.013.
Values may be sent and summed in bfloat16 or wider, within the bound.
A program may use at most 128 MiB of HBM per device.

```python
import math
import jax
import jax.numpy as jnp
import numpy as np
from jax import lax

D = 512
CH = 227
LAYERS = 2
GRID_DEV = 256
MESH_DEV = 256
EDGES_DEV = 2048
BORDER = 32
PARTITIONS = 16
CAP = 32
GRID = 4096
MESH = 4096
EDGES = 32768


def set_ends(drawn, own_key, low, high):
    shape = drawn.shape
    place = [jax.random.randint(jax.random.fold_in(own_key, axis), (), 0, shape[axis]) for axis in range(len(shape))]
    drawn = drawn.at[tuple(place)].set(low)
    longest = shape.index(max(shape))
    place[longest] = (place[longest] + 1) % shape[longest]
    return drawn.at[tuple(place)].set(high)


def block_levels(own_key, shape, pieces, low, largest):
    factor_of = 1.0
    for position, parts in pieces:
        draws = jax.random.uniform(jax.random.fold_in(jax.random.fold_in(own_key, 6), position), (parts,), jnp.float32, low / len(pieces), largest / len(pieces))
        factor_of = factor_of * jnp.repeat(jnp.exp(draws), shape[position] // parts).reshape((-1,) + (1,) * (len(shape) - 1 - position))
    return factor_of


def assign_block(key, own, number, rows, count, top, bound, skew):
    order = jax.random.permutation(key, count)
    crowded, ordinary = portions_of(count, rows * top, bound, skew, True), portions_of(count, rows * top, bound, skew, False)
    places = jnp.arange(count)

    def named(lengths, turn):
        used = int((lengths > 0).sum())
        fixed = max(1, used // 4)
        shifted = fixed + (places - fixed + turn * (used - fixed)) % max(1, count - fixed)
        return jnp.zeros((count,), jnp.int32).at[order[jnp.where(places < fixed, places, shifted)]].set(jnp.asarray(lengths, jnp.int32))

    lengths = jnp.where(number % 4 == 0, named(crowded, number // 4), named(ordinary, number - number // 4 - 1))
    mixed = jax.random.permutation(jax.random.fold_in(own, 3), count)
    donor, taker = mixed[0:count // 2 * 2:2], mixed[1:count // 2 * 2:2]
    room = jnp.minimum(lengths[donor] - 1, bound - lengths[taker]) // 2
    room = jnp.where((donor == order[0]) | (taker == order[0]) | (lengths[taker] == 0), 0, jnp.maximum(room, 0))
    shifted = jax.random.randint(jax.random.fold_in(own, 4), (count // 2,), 0, 1 << 20) % (room + 1)
    lengths = lengths.at[donor].add(-shifted).at[taker].add(shifted)
    labels = jnp.searchsorted(jnp.cumsum(lengths), jnp.arange(rows * top), side="right").astype(jnp.int32)
    grid = labels.reshape(top, rows).T
    grid = grid[jax.random.permutation(jax.random.fold_in(own, 1), rows)]
    turn = jax.random.randint(jax.random.fold_in(own, 2), (rows, 1), 0, top)
    return jnp.take_along_axis(grid, (jnp.arange(top)[None, :] + turn) % top, axis=1)


def portions_of(number_of, total, limit, skew, full):
    loads = [(1 << 20) // math.isqrt(rank ** skew) + 1 for rank in range(1, number_of + 1)]
    largest = limit if full else min(limit, max(-(-total // number_of), total * loads[0] // sum(loads)))
    least = 1 if total - largest >= number_of - 1 else 0
    holding, spare = [largest] + [least] * (number_of - 1), total - largest - least * (number_of - 1)
    while spare > 0:
        free = [i for i in range(1, number_of) if holding[i] < largest] or [i for i in range(1, number_of) if holding[i] < limit]
        mass, remaining = sum([loads[i] for i in free]), spare
        for i in free:
            extra = min(limit - holding[i], max(1, remaining * loads[i] // mass), spare)
            holding[i] = holding[i] + extra
            spare = spare - extra
    return np.array(holding)


def bell_draw(rng, dims, spread, reach, pieces=(), held_as=jnp.bfloat16):
    entries = spread * jax.random.normal(rng, dims, jnp.float32)
    if pieces:
        entries = entries * block_levels(rng, dims, pieces, -0.22, 0.18)
    return jnp.clip(entries, -reach, reach).astype(held_as)


def setup_inputs(seed: int = 0, part: int = 0) -> dict:
    keys = jax.random.split(jax.random.key(seed), 22)
    part_splits = jax.random.split(jax.random.fold_in(keys[21], part), 22)
    grid_feats = bell_draw(part_splits[0], (GRID, CH), 1.0, 6.0, ((0, 16),))
    mesh_feat = bell_draw(keys[1], (MESH, D), 1.0, 6.0, ((0, 16),))
    edge_latent = bell_draw(keys[2], (EDGES, D), 1.0, 6.0, ((0, 16),))
    g2m_owner_keys = jax.random.split(jax.random.fold_in(keys[3], 1), GRID // GRID_DEV)
    g2m_owner_turns = jax.random.permutation(jax.random.fold_in(keys[3], 3), GRID // GRID_DEV)
    g2m_owner = jax.vmap(lambda own, number: assign_block(jax.random.fold_in(keys[3], 2), own, number, GRID_DEV, PARTITIONS, 1, CAP, 2))(g2m_owner_keys, g2m_owner_turns).reshape((GRID, 1))
    g2m_node = set_ends(jax.random.randint(keys[4], (GRID,), 0, MESH_DEV), jax.random.fold_in(keys[4], 1), 0, MESH_DEV - 1).astype(jnp.int32)
    edge_sender = set_ends(jax.random.randint(keys[5], (EDGES,), 0, MESH_DEV + 2 * BORDER), jax.random.fold_in(keys[5], 1), 0, (MESH_DEV + 2 * BORDER) - 1).astype(jnp.int32)
    edge_receiver = set_ends(jax.random.randint(keys[6], (EDGES,), 0, MESH_DEV), jax.random.fold_in(keys[6], 1), 0, MESH_DEV - 1).astype(jnp.int32)
    border_low = set_ends(jax.random.randint(keys[7], (PARTITIONS, BORDER), 0, MESH_DEV), jax.random.fold_in(keys[7], 1), 0, MESH_DEV - 1).astype(jnp.int32)
    border_high = set_ends(jax.random.randint(keys[8], (PARTITIONS, BORDER), 0, MESH_DEV), jax.random.fold_in(keys[8], 1), 0, MESH_DEV - 1).astype(jnp.int32)
    w_embed = bell_draw(keys[9], (CH, D), CH ** -0.5, 0.375)
    w_g2m = bell_draw(keys[10], (D, D), D ** -0.5, 0.25)
    gain_enc = jnp.clip(1.0 + 0.18 * jax.random.normal(keys[11], (D,), jnp.float32), 0.1, 1.9)
    w_edge_in = bell_draw(keys[12], (LAYERS, 3 * D, D), (3 * D) ** -0.5, 0.15625)
    w_edge_out = bell_draw(keys[13], (LAYERS, D, D), D ** -0.5, 0.25)
    gain_edge = jnp.clip(1.0 + 0.18 * jax.random.normal(keys[14], (LAYERS, D), jnp.float32), 0.1, 1.9)
    w_node_in = bell_draw(keys[15], (LAYERS, 2 * D, D), (2 * D) ** -0.5, 0.1875)
    w_node_out = bell_draw(keys[16], (LAYERS, D, D), D ** -0.5, 0.25)
    gain_node = jnp.clip(1.0 + 0.18 * jax.random.normal(keys[17], (LAYERS, D), jnp.float32), 0.1, 1.9)
    w_m2g_mesh = bell_draw(keys[18], (D, D), D ** -0.5, 0.25)
    w_m2g_grid = bell_draw(keys[19], (D, D), D ** -0.5, 0.25)
    w_out = bell_draw(keys[20], (D, CH), D ** -0.5, 0.25)
    return dict(grid_feats=grid_feats, mesh_feat=mesh_feat, edge_latent=edge_latent, g2m_owner=g2m_owner, g2m_node=g2m_node, edge_sender=edge_sender, edge_receiver=edge_receiver, border_low=border_low, border_high=border_high, w_embed=w_embed, w_g2m=w_g2m, gain_enc=gain_enc, w_edge_in=w_edge_in, w_edge_out=w_edge_out, gain_edge=gain_edge, w_node_in=w_node_in, w_node_out=w_node_out, gain_node=gain_node, w_m2g_mesh=w_m2g_mesh, w_m2g_grid=w_m2g_grid, w_out=w_out)


def rms_norm(values, gain):
    return values * lax.rsqrt(lax.optimization_barrier(jnp.mean(values * values, -1, keepdims=True)) + 1e-05) * gain

def reference(grid_feats, mesh_feat, edge_latent, g2m_owner, g2m_node, edge_sender, edge_receiver, border_low, border_high, w_embed, w_g2m, gain_enc, w_edge_in, w_edge_out, gain_edge, w_node_in, w_node_out, gain_node, w_m2g_mesh, w_m2g_grid, w_out):
    f32 = jnp.float32
    bf16 = jnp.bfloat16
    grid_latent = jax.nn.silu(jnp.dot(grid_feats, w_embed, preferred_element_type=f32)).astype(bf16)
    target = (g2m_owner[:, 0] * MESH_DEV + g2m_node).astype(jnp.int32)
    encoded = jax.ops.segment_sum(grid_latent.astype(f32), target, num_segments=MESH).astype(bf16)
    mesh_state = (mesh_feat.astype(f32) + rms_norm(jnp.dot(encoded, w_g2m, preferred_element_type=f32), gain_enc)).astype(bf16)
    edge_part = (jnp.arange(EDGES, dtype=jnp.int32) // EDGES_DEV).astype(jnp.int32)
    sender = edge_sender
    own_node = sender < MESH_DEV
    from_prev = (sender >= MESH_DEV) & (sender < MESH_DEV + BORDER)
    prev_part = jnp.clip(edge_part - 1, 0, PARTITIONS - 1)
    next_part = jnp.clip(edge_part + 1, 0, PARTITIONS - 1)
    prev_node = border_high[prev_part, jnp.clip(sender - MESH_DEV, 0, BORDER - 1)]
    next_node = border_low[next_part, jnp.clip(sender - MESH_DEV - BORDER, 0, BORDER - 1)]
    sender_global = jnp.where(own_node, edge_part * MESH_DEV + sender, jnp.where(from_prev, prev_part * MESH_DEV + prev_node, next_part * MESH_DEV + next_node)).astype(jnp.int32)
    valid = own_node | from_prev & (edge_part > 0) | (sender >= MESH_DEV + BORDER) & (edge_part < PARTITIONS - 1)
    receiver_global = (edge_part * MESH_DEV + edge_receiver).astype(jnp.int32)
    edges_now = edge_latent
    for depth in range(LAYERS):
        sender_rows = jnp.where(valid[:, None], mesh_state[sender_global], jnp.zeros((), bf16))
        receiver_rows = mesh_state[receiver_global]
        edge_weight = w_edge_in[depth]
        pre_act = jnp.dot(edges_now, edge_weight[:D], preferred_element_type=f32) + jnp.dot(sender_rows, edge_weight[D:2 * D], preferred_element_type=f32) + jnp.dot(receiver_rows, edge_weight[2 * D:], preferred_element_type=f32)
        edge_hidden = jax.nn.silu(pre_act).astype(bf16)
        edges_now = (edges_now.astype(f32) + rms_norm(jnp.dot(edge_hidden, w_edge_out[depth], preferred_element_type=f32), gain_edge[depth])).astype(bf16)
        edge_sum = jax.ops.segment_sum(edges_now.astype(f32), receiver_global, num_segments=MESH).astype(bf16)
        node_weight = w_node_in[depth]
        node_pre = jnp.dot(mesh_state, node_weight[:D], preferred_element_type=f32) + jnp.dot(edge_sum, node_weight[D:], preferred_element_type=f32)
        node_hidden = jax.nn.silu(node_pre).astype(bf16)
        mesh_state = (mesh_state.astype(f32) + rms_norm(jnp.dot(node_hidden, w_node_out[depth], preferred_element_type=f32), gain_node[depth])).astype(bf16)
    mesh_term = jnp.dot(mesh_state, w_m2g_mesh, preferred_element_type=f32).astype(bf16)
    fetched = mesh_term[target]
    decoded = jax.nn.silu(fetched.astype(f32) + jnp.dot(grid_latent, w_m2g_grid, preferred_element_type=f32)).astype(bf16)
    return (grid_feats.astype(f32) + jnp.dot(decoded, w_out, preferred_element_type=f32)).astype(bf16)
```

```python
import functools

import jax
import jax.numpy as jnp
from jax import lax
from jax.experimental import pallas as pl
from jax.experimental.pallas import tpu as pltpu
from jax.sharding import PartitionSpec as P

F32 = jnp.float32
BF16 = jnp.bfloat16
MESH_ID = pl.DeviceIdType.MESH


def mm(a, b):
    return jnp.dot(a, b, preferred_element_type=F32)


def silu(v):
    return (0.5 * v) * (1.0 + jnp.tanh(0.5 * v))


def rms_norm(values, gain):
    return values * lax.rsqrt(jnp.mean(values * values, -1, keepdims=True) + 1e-05) * gain


def hot(condition):
    return jnp.where(condition, 1.0, 0.0).astype(BF16)


def iota(shape, axis):
    return lax.broadcasted_iota(jnp.int32, shape, axis)


def kernel(
    sizes,
    feats,
    owner,
    node,
    sender,
    receiver,
    low,
    high,
    gain_enc,
    gain_edge,
    gain_node,
    w_embed,
    w_out,
    mesh_feat_hbm,
    edge_hbm,
    w_g2m_hbm,
    w_edge_in_hbm,
    w_edge_out_hbm,
    w_node_in_hbm,
    w_node_out_hbm,
    w_mm_hbm,
    w_mg_hbm,
    out,
    x_pad,
    emb_pad,
    out_pad,
    mesh_feat,
    edges,
    w_g2m,
    w_edge_in,
    w_edge_out,
    w_node_in,
    w_node_out,
    w_mm,
    w_mg,
    send,
    recv,
    reply,
    back,
    unpack,
    gterm,
    pre,
    onehot,
    rhot,
    table,
    border,
    total,
    state,
    load_sem,
    a_send,
    a_recv,
    b_send,
    b_recv,
    h_send,
    h_recv,
):
    n, cap, chunk, tile = sizes
    me = lax.axis_index("band")
    grid_rows, channels = feats.shape
    width = x_pad.shape[1]
    mesh_rows, latent = mesh_feat.shape
    layers = w_edge_in.shape[0]
    slots = n * cap
    peers = chunk // cap
    rim = low.shape[1]
    tiles = edges.shape[0] // tile
    own0 = mesh_rows
    prev0 = 2 * mesh_rows
    next0 = prev0 + rim

    table[:, prev0:, :] = jnp.zeros(
        (layers, table.shape[1] - prev0, latent), BF16
    )

    barrier = pltpu.get_barrier_semaphore()

    def greet(k, c):
        pl.semaphore_signal(
            barrier,
            inc=1,
            device_id={"band": lax.rem(me + k, n)},
            device_id_type=MESH_ID,
        )
        return c

    lax.fori_loop(1, n, greet, 0)

    loads = [
        pltpu.make_async_copy(src, dst, load_sem.at[i])
        for i, (src, dst) in enumerate(
            (
                (w_edge_in_hbm, w_edge_in),
                (edge_hbm, edges),
                (w_g2m_hbm, w_g2m),
                (mesh_feat_hbm, mesh_feat),
                (w_edge_out_hbm, w_edge_out),
                (w_node_in_hbm, w_node_in),
                (w_node_out_hbm, w_node_out),
                (w_mg_hbm, w_mg),
                (w_mm_hbm, w_mm),
            )
        )
    ]
    for load in loads:
        load.start()

    owner_row = owner[...]
    owner_hot = owner_row == iota((n, grid_rows), 0)
    before = hot(iota((grid_rows, grid_rows), 0) < iota((grid_rows, grid_rows), 1))
    ranks = mm(hot(owner_hot), before)
    rank_row = jnp.sum(jnp.where(owner_hot, ranks, 0.0), 0, keepdims=True)
    flat_row = owner_row * cap + rank_row.astype(jnp.int32)
    flat_col = jnp.transpose(
        jnp.broadcast_to(flat_row.astype(F32), (8, grid_rows))
    )[:, 0:1]
    node_col = jnp.transpose(
        jnp.broadcast_to(node[...].astype(F32), (8, grid_rows))
    )[:, 0:1]
    x_pad[...] = jnp.zeros(x_pad.shape, BF16)
    x_pad[:, :channels] = feats[...]
    rows = jnp.where(
        iota((grid_rows, width), 1) == channels, node_col + 1.0, x_pad[...].astype(F32)
    ).astype(BF16)
    for c in range(slots // chunk):
        pick = hot(iota((chunk, grid_rows), 0) + c * chunk == flat_row)
        send[c * peers : (c + 1) * peers] = (
            mm(pick, rows).astype(BF16).reshape(peers, cap, width)
        )

    pl.semaphore_wait(barrier, n - 1)

    def to_owner(k):
        peer = lax.rem(me + k, n)
        return pltpu.make_async_remote_copy(
            src_ref=send.at[peer],
            dst_ref=recv.at[me],
            send_sem=a_send.at[peer],
            recv_sem=a_recv.at[me],
            device_id={"band": peer},
            device_id_type=MESH_ID,
        )

    def from_source(k):
        peer = lax.rem(me + k, n)
        return pltpu.make_async_remote_copy(
            src_ref=send.at[me],
            dst_ref=recv.at[peer],
            send_sem=a_send.at[me],
            recv_sem=a_recv.at[peer],
            device_id={"band": peer},
            device_id_type=MESH_ID,
        )

    def start_a(k, c):
        to_owner(k).start()
        return c

    lax.fori_loop(1, n, start_a, 0)
    recv[me] = send[me]

    unpack[...] = hot(iota((grid_rows, slots), 1).astype(F32) == flat_col)
    emb_pad[...] = jnp.zeros(emb_pad.shape, BF16)
    emb_pad[:channels, :] = w_embed[...]
    out_pad[...] = jnp.zeros(out_pad.shape, BF16)
    out_pad[:, :channels] = w_out[...]

    send_cols = jnp.transpose(sender[...].astype(F32))
    recv_cols = jnp.transpose(receiver[...].astype(F32))
    lanes = send_cols.shape[0]
    spare = onehot.shape[1] - mesh_rows
    lane_r = iota((lanes, mesh_rows), 1).astype(F32)
    lane_s = iota((lanes, spare), 1).astype(F32)
    for j in range(send_cols.shape[1]):
        at = slice(j * lanes, (j + 1) * lanes)
        onehot[at, :mesh_rows] = hot(recv_cols[:, j : j + 1] == lane_r)
        onehot[at, mesh_rows:] = hot(send_cols[:, j : j + 1] == lane_s)
    per = tile // lanes
    sub = iota((mesh_rows, lanes), 0)
    for j in range(send_cols.shape[1]):
        rhot[j // per, :, (j % per) * lanes : (j % per + 1) * lanes] = hot(
            receiver[j : j + 1, :] == sub
        )

    square = iota((rim, rim), 0) == iota((rim, rim), 1)
    low_col = jnp.sum(jnp.where(square, low[...].astype(F32), 0.0), 1, keepdims=True)
    high_col = jnp.sum(jnp.where(square, high[...].astype(F32), 0.0), 1, keepdims=True)
    rim_lane = iota((rim, mesh_rows), 1).astype(F32)
    low_hot = hot(low_col == rim_lane)
    high_hot = hot(high_col == rim_lane)

    loads[0].wait()
    loads[1].wait()

    def own_term(depth):
        def body(t, c):
            at = pl.ds(pl.multiple_of(t * tile, tile), tile)
            pre[at, :] = mm(edges[at, :], w_edge_in[depth, :latent, :])
            return c

        lax.fori_loop(0, tiles, body, 0)

    own_term(0)
    for load in loads[2:]:
        load.wait()

    def arrive_a(k, c):
        from_source(k).wait_recv()
        return c

    lax.fori_loop(1, n, arrive_a, 0)

    mark = hot(iota((16, width), 1) == channels)
    total[...] = jnp.zeros(total.shape, F32)

    def block(c):
        return recv[pl.ds(c * peers, peers)].reshape(chunk, width)

    for c in range(slots // chunk):
        got = block(c)
        ids = lax.dot_general(
            mark, got, (((1,), (1,)), ((), ())), preferred_element_type=F32
        )[0:1, :]
        pick = hot(ids == (iota((mesh_rows, chunk), 0) + 1).astype(F32))
        lat = silu(mm(got, emb_pad[...])).astype(BF16)
        gterm[c * chunk : (c + 1) * chunk, :] = lat
        total[...] += mm(pick, lat)
    encoded = total[...].astype(BF16)
    state[...] = (
        mesh_feat[...].astype(F32) + rms_norm(mm(encoded, w_g2m[...]), gain_enc[...])
    ).astype(BF16)

    def border_copy(depth, up):
        peer = lax.rem(me + 1, n) if up else lax.rem(me + n - 1, n)
        first = prev0 if up else next0
        return pltpu.make_async_remote_copy(
            src_ref=border.at[depth, int(up)],
            dst_ref=table.at[depth, pl.ds(first, rim)],
            send_sem=h_send.at[depth, int(up)],
            recv_sem=h_recv.at[depth, int(up)],
            device_id={"band": peer},
            device_id_type=MESH_ID,
        )

    for depth in range(layers):
        own = mm(state[...], w_edge_in[depth, latent : 2 * latent, :]).astype(BF16)
        border[depth, 0] = mm(low_hot, own).astype(BF16)
        border[depth, 1] = mm(high_hot, own).astype(BF16)

        @pl.when(me < n - 1)
        def _():
            border_copy(depth, True).start()

        @pl.when(me > 0)
        def _():
            border_copy(depth, False).start()

        table[depth, own0:prev0, :] = own
        table[depth, :own0, :] = mm(
            state[...], w_edge_in[depth, 2 * latent :, :]
        ).astype(BF16)
        if depth > 0:
            own_term(depth)
        total[...] = jnp.zeros(total.shape, F32)

        @pl.when(me > 0)
        def _():
            border_copy(depth, True).wait_recv()

        @pl.when(me < n - 1)
        def _():
            border_copy(depth, False).wait_recv()

        def edge_step(t, c):
            at = pl.ds(pl.multiple_of(t * tile, tile), tile)
            hidden = silu(pre[at, :] + mm(onehot[at, :], table[depth])).astype(BF16)
            now = (
                edges[at, :].astype(F32)
                + rms_norm(mm(hidden, w_edge_out[depth]), gain_edge[depth : depth + 1, :])
            ).astype(BF16)
            if depth < layers - 1:
                edges[at, :] = now
            total[...] += mm(rhot[t], now)
            return c

        lax.fori_loop(0, tiles, edge_step, 0)
        summed = total[...].astype(BF16)
        hidden = silu(
            mm(state[...], w_node_in[depth, :latent, :])
            + mm(summed, w_node_in[depth, latent:, :])
        ).astype(BF16)
        state[...] = (
            state[...].astype(F32)
            + rms_norm(mm(hidden, w_node_out[depth]), gain_node[depth : depth + 1, :])
        ).astype(BF16)

    term = mm(state[...], w_mm[...]).astype(BF16)

    def to_source(peer):
        return pltpu.make_async_remote_copy(
            src_ref=reply.at[peer],
            dst_ref=back.at[me],
            send_sem=b_send.at[peer],
            recv_sem=b_recv.at[me],
            device_id={"band": peer},
            device_id_type=MESH_ID,
        )

    def from_owner(peer):
        return pltpu.make_async_remote_copy(
            src_ref=reply.at[me],
            dst_ref=back.at[peer],
            send_sem=b_send.at[me],
            recv_sem=b_recv.at[peer],
            device_id={"band": peer},
            device_id_type=MESH_ID,
        )

    for c in range(slots // chunk):
        got = block(c).astype(F32)
        pick = hot(
            got[:, channels : channels + 1] == (iota((chunk, mesh_rows), 1) + 1).astype(F32)
        )
        lat = gterm[c * chunk : (c + 1) * chunk, :]
        dec = silu(mm(pick, term) + mm(lat, w_mg[...])).astype(BF16)
        reply[c * peers : (c + 1) * peers] = (
            (got + mm(dec, out_pad[...])).astype(BF16).reshape(peers, cap, width)
        )

        def start_b(peer, k):
            @pl.when(peer != me)
            def _():
                to_source(peer).start()

            return k

        lax.fori_loop(c * peers, (c + 1) * peers, start_b, 0)
    back[me] = reply[me]

    def arrive_b(k, c):
        from_owner(lax.rem(me + k, n)).wait_recv()
        return c

    lax.fori_loop(1, n, arrive_b, 0)
    result = mm(unpack[...], back[...].reshape(slots, width)).astype(BF16)
    out[...] = result[:, :channels]

    def sent(k, c):
        to_owner(k).wait_send()
        to_source(lax.rem(me + k, n)).wait_send()
        return c

    lax.fori_loop(1, n, sent, 0)
    for depth in range(layers):

        @pl.when(me < n - 1)
        def _():
            border_copy(depth, True).wait_send()

        @pl.when(me > 0)
        def _():
            border_copy(depth, False).wait_send()


def round_up(value, step):
    return -(-value // step) * step


def shards(
    grid_feats,
    mesh_feat,
    edge_latent,
    g2m_owner,
    g2m_node,
    edge_sender,
    edge_receiver,
    border_low,
    border_high,
    w_embed,
    w_g2m,
    gain_enc,
    w_edge_in,
    w_edge_out,
    gain_edge,
    w_node_in,
    w_node_out,
    gain_node,
    w_m2g_mesh,
    w_m2g_grid,
    w_out,
):
    n = lax.axis_size("band")
    grid_rows, channels = grid_feats.shape
    mesh_rows, latent = mesh_feat.shape
    edge_rows = edge_latent.shape[0]
    layers = w_edge_in.shape[0]
    rim = border_low.shape[1]
    cap = round_up(2 * grid_rows // n, 16)
    slots = n * cap
    chunk = min(slots, 256)
    tile = min(edge_rows, 512)
    width = round_up(channels + 1, 128)
    table_rows = round_up(2 * mesh_rows + 2 * rim, 128)
    vmem = pl.BlockSpec(memory_space=pltpu.VMEM)
    hbm = pl.BlockSpec(memory_space=pl.ANY)

    def like(a):
        return pltpu.VMEM(a.shape, a.dtype)

    dma = pltpu.SemaphoreType.DMA
    return pl.pallas_call(
        functools.partial(kernel, (n, cap, chunk, tile)),
        out_shape=jax.ShapeDtypeStruct((grid_rows, channels), BF16),
        in_specs=[vmem] * 12 + [hbm] * 9,
        out_specs=vmem,
        scratch_shapes=[
            pltpu.VMEM((grid_rows, width), BF16),
            pltpu.VMEM((width, latent), BF16),
            pltpu.VMEM((latent, width), BF16),
            like(mesh_feat),
            like(edge_latent),
            like(w_g2m),
            like(w_edge_in),
            like(w_edge_out),
            like(w_node_in),
            like(w_node_out),
            like(w_m2g_mesh),
            like(w_m2g_grid),
            pltpu.VMEM((n, cap, width), BF16),
            pltpu.VMEM((n, cap, width), BF16),
            pltpu.VMEM((n, cap, width), BF16),
            pltpu.VMEM((n, cap, width), BF16),
            pltpu.VMEM((grid_rows, slots), BF16),
            pltpu.VMEM((slots, latent), BF16),
            pltpu.VMEM((edge_rows, latent), F32),
            pltpu.VMEM((edge_rows, table_rows), BF16),
            pltpu.VMEM((edge_rows // tile, mesh_rows, tile), BF16),
            pltpu.VMEM((layers, table_rows, latent), BF16),
            pltpu.VMEM((layers, 2, rim, latent), BF16),
            pltpu.VMEM((mesh_rows, latent), F32),
            pltpu.VMEM((mesh_rows, latent), BF16),
            dma((9,)),
            dma((n,)),
            dma((n,)),
            dma((n,)),
            dma((n,)),
            dma((layers, 2)),
            dma((layers, 2)),
        ],
        compiler_params=pltpu.CompilerParams(
            collective_id=0, has_side_effects=True, vmem_limit_bytes=56 * 1024 * 1024
        ),
        cost_estimate=pl.CostEstimate(
            flops=10_000_000_000, bytes_accessed=16_000_000, transcendentals=3_000_000
        ),
    )(
        grid_feats,
        g2m_owner.reshape(1, grid_rows),
        g2m_node.reshape(1, grid_rows),
        edge_sender.reshape(edge_rows // 128, 128),
        edge_receiver.reshape(edge_rows // 128, 128),
        border_low,
        border_high,
        gain_enc.reshape(1, latent),
        gain_edge,
        gain_node,
        w_embed,
        w_out,
        mesh_feat,
        edge_latent,
        w_g2m,
        w_edge_in,
        w_edge_out,
        w_node_in,
        w_node_out,
        w_m2g_mesh,
        w_m2g_grid,
    )


def solution(mesh):
    return jax.shard_map(
        shards,
        mesh=mesh,
        in_specs=(
            P(("groups", "band"), None),
            P("band", None),
            P("band", None),
            P("band", None),
            P("band"),
            P("band"),
            P("band"),
            P("band", None),
            P("band", None),
        )
        + (P(),) * 12,
        out_specs=P(("groups", "band"), None),
        check_vma=False,
    )
```

```python
import functools

import jax
import jax.numpy as jnp
from jax import lax
from jax.experimental import pallas as pl
from jax.experimental.pallas import tpu as pltpu
from jax.sharding import PartitionSpec as P

F32 = jnp.float32
BF16 = jnp.bfloat16
MESH_ID = pl.DeviceIdType.MESH


def mm(a, b):
    return jnp.dot(a, b, preferred_element_type=F32)


def mm_t(a, b):
    return lax.dot_general(a, b, (((1,), (1,)), ((), ())), preferred_element_type=F32)


def silu(v):
    return (0.5 * v) * (1.0 + jnp.tanh(0.5 * v))


def rms_norm(values, gain):
    return values * lax.rsqrt(jnp.mean(values * values, -1, keepdims=True) + 1e-05) * gain


def hot(condition):
    return jnp.where(condition, 1.0, 0.0).astype(BF16)


def iota(shape, axis):
    return lax.broadcasted_iota(jnp.int32, shape, axis)


def kernel(
    sizes,
    feats,
    owner,
    node,
    sender,
    receiver,
    low,
    high,
    gain_enc,
    gain_edge,
    gain_node,
    w_embed,
    w_out,
    mesh_feat_hbm,
    edge_hbm,
    w_g2m_hbm,
    w_edge_in_hbm,
    w_edge_out_hbm,
    w_node_in_hbm,
    w_node_out_hbm,
    w_mm_hbm,
    w_mg_hbm,
    out,
    x_pad,
    emb_pad,
    out_pad,
    mesh_feat,
    edges,
    w_g2m,
    w_edge_in,
    w_edge_out,
    w_node_in,
    w_node_out,
    w_mm,
    w_mg,
    send,
    recv,
    reply,
    back,
    unpack,
    lats,
    gterm,
    pre,
    onehot,
    rhot,
    table,
    border,
    total,
    state,
    load_sem,
    a_send,
    a_recv,
    b_send,
    b_recv,
    h_send,
    h_recv,
):
    n, cap, chunk, tile = sizes
    me = lax.axis_index("band")
    channels, grid_rows = feats.shape
    width = x_pad.shape[0]
    mesh_rows, latent = mesh_feat.shape
    layers = w_edge_in.shape[0]
    slots = n * cap
    peers = chunk // cap
    rim = low.shape[1]
    tiles = edges.shape[0] // tile
    own0 = mesh_rows
    prev0 = 2 * mesh_rows
    next0 = prev0 + rim

    table[:, prev0:, :] = jnp.zeros(
        (layers, table.shape[1] - prev0, latent), BF16
    )

    barrier = pltpu.get_barrier_semaphore()

    def greet(k, c):
        pl.semaphore_signal(
            barrier,
            inc=1,
            device_id={"band": lax.rem(me + k, n)},
            device_id_type=MESH_ID,
        )
        return c

    lax.fori_loop(1, n, greet, 0)

    loads = [
        pltpu.make_async_copy(src, dst, load_sem.at[i])
        for i, (src, dst) in enumerate(
            (
                (w_edge_in_hbm, w_edge_in),
                (edge_hbm, edges),
                (w_g2m_hbm, w_g2m),
                (mesh_feat_hbm, mesh_feat),
                (w_edge_out_hbm, w_edge_out),
                (w_node_in_hbm, w_node_in),
                (w_node_out_hbm, w_node_out),
                (w_mg_hbm, w_mg),
                (w_mm_hbm, w_mm),
            )
        )
    ]
    for load in loads:
        load.start()

    owner_row = owner[...]
    owner_hot = owner_row == iota((n, grid_rows), 0)
    before = hot(iota((grid_rows, grid_rows), 0) < iota((grid_rows, grid_rows), 1))
    ranks = mm(hot(owner_hot), before)
    rank_row = jnp.sum(jnp.where(owner_hot, ranks, 0.0), 0, keepdims=True)
    flat_row = owner_row * cap + rank_row.astype(jnp.int32)
    flat_col = jnp.transpose(
        jnp.broadcast_to(flat_row.astype(F32), (8, grid_rows))
    )[:, 0:1]
    x_pad[...] = jnp.zeros(x_pad.shape, BF16)
    x_pad[:channels, :] = feats[...]
    columns = jnp.where(
        iota((width, grid_rows), 0) == channels,
        node[...].astype(F32) + 1.0,
        x_pad[...].astype(F32),
    ).astype(BF16)
    for c in range(slots // chunk):
        pick = hot(iota((chunk, grid_rows), 0) + c * chunk == flat_row)
        send[c * peers : (c + 1) * peers] = (
            mm_t(pick, columns).astype(BF16).reshape(peers, cap, width)
        )

    pl.semaphore_wait(barrier, n - 1)

    half = n // 2

    def partner(k):
        far = lax.rem((me // half + 1) * half + lax.rem(me + k, half), n)
        near = (me // half) * half + lax.rem(me + k - half, half)
        return jnp.where(k < half, far, near)

    def to_owner(k):
        peer = partner(k)
        return pltpu.make_async_remote_copy(
            src_ref=send.at[peer],
            dst_ref=recv.at[me],
            send_sem=a_send.at[peer],
            recv_sem=a_recv.at[me],
            device_id={"band": peer},
            device_id_type=MESH_ID,
        )

    def from_source(k):
        peer = partner(k)
        return pltpu.make_async_remote_copy(
            src_ref=send.at[me],
            dst_ref=recv.at[peer],
            send_sem=a_send.at[me],
            recv_sem=a_recv.at[peer],
            device_id={"band": peer},
            device_id_type=MESH_ID,
        )

    def others(step):
        lax.fori_loop(0, half, step, 0)
        lax.fori_loop(half + 1, n, step, 0)

    def start_a(k, c):
        to_owner(k).start()
        return c

    others(start_a)
    recv[me] = send[me]

    unpack[...] = hot(iota((grid_rows, slots), 1).astype(F32) == flat_col)
    emb_pad[...] = jnp.zeros(emb_pad.shape, BF16)
    emb_pad[:channels, :] = w_embed[...]
    out_pad[...] = jnp.zeros(out_pad.shape, BF16)
    out_pad[:channels, :] = w_out[...]

    send_cols = jnp.transpose(sender[...].astype(F32))
    recv_cols = jnp.transpose(receiver[...].astype(F32))
    lanes = send_cols.shape[0]
    spare = onehot.shape[1] - mesh_rows
    lane_r = iota((lanes, mesh_rows), 1).astype(F32)
    lane_s = iota((lanes, spare), 1).astype(F32)
    for j in range(send_cols.shape[1]):
        at = slice(j * lanes, (j + 1) * lanes)
        onehot[at, :mesh_rows] = hot(recv_cols[:, j : j + 1] == lane_r)
        onehot[at, mesh_rows:] = hot(send_cols[:, j : j + 1] == lane_s)
    per = tile // lanes
    sub = iota((mesh_rows, lanes), 0)
    for j in range(send_cols.shape[1]):
        rhot[j // per, :, (j % per) * lanes : (j % per + 1) * lanes] = hot(
            receiver[j : j + 1, :] == sub
        )

    square = iota((rim, rim), 0) == iota((rim, rim), 1)
    low_col = jnp.sum(jnp.where(square, low[...].astype(F32), 0.0), 1, keepdims=True)
    high_col = jnp.sum(jnp.where(square, high[...].astype(F32), 0.0), 1, keepdims=True)
    rim_lane = iota((rim, mesh_rows), 1).astype(F32)
    low_hot = hot(low_col == rim_lane)
    high_hot = hot(high_col == rim_lane)

    loads[0].wait()
    loads[1].wait()

    def own_term(depth):
        def body(t, c):
            at = pl.ds(pl.multiple_of(t * tile, tile), tile)
            pre[at, :] = mm(edges[at, :], w_edge_in[depth, :latent, :])
            return c

        lax.fori_loop(0, tiles, body, 0)

    def inner_term(depth):
        def body(t, c):
            at = pl.ds(pl.multiple_of(t * tile, tile), tile)
            inner = mm(onehot[at, :prev0], table[depth, :prev0, :])
            if depth == 0:
                pre[at, :] += inner
            else:
                pre[at, :] = inner + mm(edges[at, :], w_edge_in[depth, :latent, :])
            return c

        lax.fori_loop(0, tiles, body, 0)

    own_term(0)

    def arrive_a(k, c):
        from_source(k).wait_recv()
        return c

    others(arrive_a)

    mark = hot(iota((16, width), 1) == channels)
    total[...] = jnp.zeros(total.shape, F32)

    def block(c):
        return recv[pl.ds(c * peers, peers)].reshape(chunk, width)

    for c in range(slots // chunk):
        got = block(c)
        ids = mm_t(mark, got)[0:1, :]
        pick = hot(ids == (iota((mesh_rows, chunk), 0) + 1).astype(F32))
        lat = silu(mm(got, emb_pad[...])).astype(BF16)
        lats[c * chunk : (c + 1) * chunk, :] = lat
        total[...] += mm(pick, lat)
    encoded = total[...].astype(BF16)
    for load in loads[2:4]:
        load.wait()
    state[...] = (
        mesh_feat[...].astype(F32) + rms_norm(mm(encoded, w_g2m[...]), gain_enc[...])
    ).astype(BF16)

    def border_copy(depth, up):
        peer = lax.rem(me + 1, n) if up else lax.rem(me + n - 1, n)
        first = prev0 if up else next0
        return pltpu.make_async_remote_copy(
            src_ref=border.at[depth, int(up)],
            dst_ref=table.at[depth, pl.ds(first, rim)],
            send_sem=h_send.at[depth, int(up)],
            recv_sem=h_recv.at[depth, int(up)],
            device_id={"band": peer},
            device_id_type=MESH_ID,
        )

    for load in loads[4:]:
        load.wait()
    for depth in range(layers):
        own = mm(state[...], w_edge_in[depth, latent : 2 * latent, :]).astype(BF16)
        border[depth, 0] = mm(low_hot, own).astype(BF16)
        border[depth, 1] = mm(high_hot, own).astype(BF16)

        @pl.when(me < n - 1)
        def _():
            border_copy(depth, True).start()

        @pl.when(me > 0)
        def _():
            border_copy(depth, False).start()

        table[depth, own0:prev0, :] = own
        table[depth, :own0, :] = mm(
            state[...], w_edge_in[depth, 2 * latent :, :]
        ).astype(BF16)
        inner_term(depth)
        if depth == 0:
            for c in range(slots // chunk):
                at = slice(c * chunk, (c + 1) * chunk)
                gterm[at, :] = mm(lats[at, :], w_mg[...])
        total[...] = jnp.zeros(total.shape, F32)

        @pl.when(me > 0)
        def _():
            border_copy(depth, True).wait_recv()

        @pl.when(me < n - 1)
        def _():
            border_copy(depth, False).wait_recv()

        def edge_step(t, c):
            at = pl.ds(pl.multiple_of(t * tile, tile), tile)
            hidden = silu(
                pre[at, :] + mm(onehot[at, prev0:], table[depth, prev0:, :])
            ).astype(BF16)
            now = (
                edges[at, :].astype(F32)
                + rms_norm(mm(hidden, w_edge_out[depth]), gain_edge[depth : depth + 1, :])
            ).astype(BF16)
            if depth < layers - 1:
                edges[at, :] = now
            total[...] += mm(rhot[t], now)
            return c

        lax.fori_loop(0, tiles, edge_step, 0)
        summed = total[...].astype(BF16)
        hidden = silu(
            mm(state[...], w_node_in[depth, :latent, :])
            + mm(summed, w_node_in[depth, latent:, :])
        ).astype(BF16)
        state[...] = (
            state[...].astype(F32)
            + rms_norm(mm(hidden, w_node_out[depth]), gain_node[depth : depth + 1, :])
        ).astype(BF16)

    term = mm(state[...], w_mm[...]).astype(BF16)

    def to_source(peer):
        return pltpu.make_async_remote_copy(
            src_ref=reply.at[peer],
            dst_ref=back.at[me],
            send_sem=b_send.at[peer],
            recv_sem=b_recv.at[me],
            device_id={"band": peer},
            device_id_type=MESH_ID,
        )

    def from_owner(peer):
        return pltpu.make_async_remote_copy(
            src_ref=reply.at[me],
            dst_ref=back.at[peer],
            send_sem=b_send.at[me],
            recv_sem=b_recv.at[peer],
            device_id={"band": peer},
            device_id_type=MESH_ID,
        )

    chunks = slots // chunk
    for step in range(chunks):
        c = lax.rem(me // peers + step + (chunks + 1) // 2, chunks)
        got = block(c).astype(F32)
        pick = hot(
            got[:, channels : channels + 1] == (iota((chunk, mesh_rows), 1) + 1).astype(F32)
        )
        at = pl.ds(pl.multiple_of(c * chunk, chunk), chunk)
        dec = silu(mm(pick, term) + gterm[at, :]).astype(BF16)
        reply[pl.ds(c * peers, peers)] = (
            (got + mm_t(dec, out_pad[...])).astype(BF16).reshape(peers, cap, width)
        )

        def start_b(j, k):
            peer = c * peers + lax.rem(me + j, peers)

            @pl.when(peer != me)
            def _():
                to_source(peer).start()

            return k

        lax.fori_loop(0, peers, start_b, 0)
    back[me] = reply[me]

    def arrive_b(k, c):
        from_owner(partner(k)).wait_recv()
        return c

    others(arrive_b)
    result = jnp.transpose(mm(unpack[...], back[...].reshape(slots, width)))
    out[...] = result.astype(BF16)[:channels, :]

    def sent(k, c):
        to_owner(k).wait_send()
        to_source(partner(k)).wait_send()
        return c

    others(sent)
    for depth in range(layers):

        @pl.when(me < n - 1)
        def _():
            border_copy(depth, True).wait_send()

        @pl.when(me > 0)
        def _():
            border_copy(depth, False).wait_send()


def round_up(value, step):
    return -(-value // step) * step


def shards(
    grid_feats,
    mesh_feat,
    edge_latent,
    g2m_owner,
    g2m_node,
    edge_sender,
    edge_receiver,
    border_low,
    border_high,
    w_embed,
    w_g2m,
    gain_enc,
    w_edge_in,
    w_edge_out,
    gain_edge,
    w_node_in,
    w_node_out,
    gain_node,
    w_m2g_mesh,
    w_m2g_grid,
    w_out,
):
    n = lax.axis_size("band")
    grid_rows, channels = grid_feats.shape
    mesh_rows, latent = mesh_feat.shape
    edge_rows = edge_latent.shape[0]
    layers = w_edge_in.shape[0]
    rim = border_low.shape[1]
    cap = round_up(2 * grid_rows // n, 16)
    slots = n * cap
    chunk = min(slots, 256)
    tile = min(edge_rows, 512)
    width = round_up(channels + 1, 128)
    table_rows = round_up(2 * mesh_rows + 2 * rim, 128)
    vmem = pl.BlockSpec(memory_space=pltpu.VMEM)
    hbm = pl.BlockSpec(memory_space=pl.ANY)

    def like(a):
        return pltpu.VMEM(a.shape, a.dtype)

    dma = pltpu.SemaphoreType.DMA
    return pl.pallas_call(
        functools.partial(kernel, (n, cap, chunk, tile)),
        out_shape=jax.ShapeDtypeStruct((channels, grid_rows), BF16),
        in_specs=[vmem] * 12 + [hbm] * 9,
        out_specs=vmem,
        scratch_shapes=[
            pltpu.VMEM((width, grid_rows), BF16),
            pltpu.VMEM((width, latent), BF16),
            pltpu.VMEM((width, latent), BF16),
            like(mesh_feat),
            like(edge_latent),
            like(w_g2m),
            like(w_edge_in),
            like(w_edge_out),
            like(w_node_in),
            like(w_node_out),
            like(w_m2g_mesh),
            like(w_m2g_grid),
            pltpu.VMEM((n, cap, width), BF16),
            pltpu.VMEM((n, cap, width), BF16),
            pltpu.VMEM((n, cap, width), BF16),
            pltpu.VMEM((n, cap, width), BF16),
            pltpu.VMEM((grid_rows, slots), BF16),
            pltpu.VMEM((slots, latent), BF16),
            pltpu.VMEM((slots, latent), F32),
            pltpu.VMEM((edge_rows, latent), F32),
            pltpu.VMEM((edge_rows, table_rows), BF16),
            pltpu.VMEM((edge_rows // tile, mesh_rows, tile), BF16),
            pltpu.VMEM((layers, table_rows, latent), BF16),
            pltpu.VMEM((layers, 2, rim, latent), BF16),
            pltpu.VMEM((mesh_rows, latent), F32),
            pltpu.VMEM((mesh_rows, latent), BF16),
            dma((9,)),
            dma((n,)),
            dma((n,)),
            dma((n,)),
            dma((n,)),
            dma((layers, 2)),
            dma((layers, 2)),
        ],
        compiler_params=pltpu.CompilerParams(
            collective_id=0, has_side_effects=True, vmem_limit_bytes=56 * 1024 * 1024
        ),
        cost_estimate=pl.CostEstimate(
            flops=10_000_000_000, bytes_accessed=16_000_000, transcendentals=3_000_000
        ),
    )(
        grid_feats.T,
        g2m_owner.reshape(1, grid_rows),
        g2m_node.reshape(1, grid_rows),
        edge_sender.reshape(edge_rows // 128, 128),
        edge_receiver.reshape(edge_rows // 128, 128),
        border_low,
        border_high,
        gain_enc.reshape(1, latent),
        gain_edge,
        gain_node,
        w_embed,
        w_out.T,
        mesh_feat,
        edge_latent,
        w_g2m,
        w_edge_in,
        w_edge_out,
        w_node_in,
        w_node_out,
        w_m2g_mesh,
        w_m2g_grid,
    ).T


def solution(mesh):
    return jax.shard_map(
        shards,
        mesh=mesh,
        in_specs=(
            P(("groups", "band"), None),
            P("band", None),
            P("band", None),
            P("band", None),
            P("band"),
            P("band"),
            P("band"),
            P("band", None),
            P("band", None),
        )
        + (P(),) * 12,
        out_specs=P(("groups", "band"), None),
        check_vma=False,
    )
```

```python
import functools

import jax
import jax.numpy as jnp
from jax import lax
from jax.experimental import pallas as pl
from jax.experimental.pallas import tpu as pltpu
from jax.sharding import PartitionSpec as P

F32 = jnp.float32
BF16 = jnp.bfloat16
MESH_ID = pl.DeviceIdType.MESH


def mm(a, b):
    return jnp.dot(a, b, preferred_element_type=F32)


def mm_t(a, b):
    return lax.dot_general(a, b, (((1,), (1,)), ((), ())), preferred_element_type=F32)


def silu(v):
    return (0.5 * v) * (1.0 + jnp.tanh(0.5 * v))


def rms_norm(values, gain):
    return values * lax.rsqrt(jnp.mean(values * values, -1, keepdims=True) + 1e-05) * gain


def hot(condition):
    return jnp.where(condition, 1.0, 0.0).astype(BF16)


def iota(shape, axis):
    return lax.broadcasted_iota(jnp.int32, shape, axis)


def kernel(
    sizes,
    feats,
    owner,
    node,
    sender,
    receiver,
    low,
    high,
    gain_enc,
    gain_edge,
    gain_node,
    w_embed,
    w_out,
    mesh_feat_hbm,
    edge_hbm,
    w_g2m_hbm,
    w_edge_in_hbm,
    w_edge_out_hbm,
    w_node_in_hbm,
    w_node_out_hbm,
    w_mm_hbm,
    w_mg_hbm,
    out,
    x_pad,
    emb_pad,
    out_pad,
    mesh_feat,
    edges,
    w_g2m,
    w_edge_in,
    w_edge_out,
    w_node_in,
    w_node_out,
    w_mm,
    w_mg,
    send,
    recv,
    reply,
    back,
    unpack,
    lats,
    gterm,
    pre,
    onehot,
    rhot,
    table,
    border,
    total,
    state,
    load_sem,
    a_send,
    a_recv,
    b_send,
    b_recv,
    h_send,
    h_recv,
):
    n, cap, chunk, tile = sizes
    me = lax.axis_index("band")
    channels, grid_rows = feats.shape
    width = x_pad.shape[0]
    mesh_rows, latent = mesh_feat.shape
    layers = w_edge_in.shape[0]
    slots = n * cap
    peers = chunk // cap
    rim = low.shape[1]
    tiles = edges.shape[0] // tile
    own0 = mesh_rows
    prev0 = 2 * mesh_rows
    next0 = prev0 + rim

    table[:, prev0:, :] = jnp.zeros(
        (layers, table.shape[1] - prev0, latent), BF16
    )

    barrier = pltpu.get_barrier_semaphore()

    def greet(k, c):
        pl.semaphore_signal(
            barrier,
            inc=1,
            device_id={"band": lax.rem(me + k, n)},
            device_id_type=MESH_ID,
        )
        return c

    lax.fori_loop(1, n, greet, 0)

    loads = [
        pltpu.make_async_copy(src, dst, load_sem.at[i])
        for i, (src, dst) in enumerate(
            (
                (w_edge_in_hbm, w_edge_in),
                (edge_hbm, edges),
                (w_g2m_hbm, w_g2m),
                (mesh_feat_hbm, mesh_feat),
                (w_edge_out_hbm, w_edge_out),
                (w_node_in_hbm, w_node_in),
                (w_node_out_hbm, w_node_out),
                (w_mg_hbm, w_mg),
                (w_mm_hbm, w_mm),
            )
        )
    ]
    for load in loads:
        load.start()

    owner_row = owner[...]
    owner_hot = owner_row == iota((n, grid_rows), 0)
    before = hot(iota((grid_rows, grid_rows), 0) < iota((grid_rows, grid_rows), 1))
    ranks = mm(hot(owner_hot), before)
    rank_row = jnp.sum(jnp.where(owner_hot, ranks, 0.0), 0, keepdims=True)
    flat_row = owner_row * cap + rank_row.astype(jnp.int32)
    flat_col = jnp.transpose(
        jnp.broadcast_to(flat_row.astype(F32), (8, grid_rows))
    )[:, 0:1]
    x_pad[...] = jnp.zeros(x_pad.shape, BF16)
    x_pad[:channels, :] = feats[...]
    columns = jnp.where(
        iota((width, grid_rows), 0) == channels,
        node[...].astype(F32) + 1.0,
        x_pad[...].astype(F32),
    ).astype(BF16)
    for c in range(slots // chunk):
        pick = hot(iota((chunk, grid_rows), 0) + c * chunk == flat_row)
        send[c * peers : (c + 1) * peers] = (
            mm_t(pick, columns).astype(BF16).reshape(peers, cap, width)
        )

    pl.semaphore_wait(barrier, n - 1)

    def partner(k):
        return lax.rem(me + k, n)

    def to_owner(k):
        peer = partner(k)
        return pltpu.make_async_remote_copy(
            src_ref=send.at[peer],
            dst_ref=recv.at[me],
            send_sem=a_send.at[peer],
            recv_sem=a_recv.at[me],
            device_id={"band": peer},
            device_id_type=MESH_ID,
        )

    def from_source(k):
        peer = partner(k)
        return pltpu.make_async_remote_copy(
            src_ref=send.at[me],
            dst_ref=recv.at[peer],
            send_sem=a_send.at[me],
            recv_sem=a_recv.at[peer],
            device_id={"band": peer},
            device_id_type=MESH_ID,
        )

    def others(step):
        lax.fori_loop(1, n, step, 0)

    def start_a(k, c):
        to_owner(k).start()
        return c

    others(start_a)
    recv[me] = send[me]

    unpack[...] = hot(iota((grid_rows, slots), 1).astype(F32) == flat_col)
    emb_pad[...] = jnp.zeros(emb_pad.shape, BF16)
    emb_pad[:channels, :] = w_embed[...]
    out_pad[...] = jnp.zeros(out_pad.shape, BF16)
    out_pad[:channels, :] = w_out[...]

    send_cols = jnp.transpose(sender[...].astype(F32))
    recv_cols = jnp.transpose(receiver[...].astype(F32))
    lanes = send_cols.shape[0]
    spare = onehot.shape[1] - mesh_rows
    lane_r = iota((lanes, mesh_rows), 1).astype(F32)
    lane_s = iota((lanes, spare), 1).astype(F32)
    for j in range(send_cols.shape[1]):
        at = slice(j * lanes, (j + 1) * lanes)
        onehot[at, :mesh_rows] = hot(recv_cols[:, j : j + 1] == lane_r)
        onehot[at, mesh_rows:] = hot(send_cols[:, j : j + 1] == lane_s)
    per = tile // lanes
    sub = iota((mesh_rows, lanes), 0)
    for j in range(send_cols.shape[1]):
        rhot[j // per, :, (j % per) * lanes : (j % per + 1) * lanes] = hot(
            receiver[j : j + 1, :] == sub
        )

    square = iota((rim, rim), 0) == iota((rim, rim), 1)
    low_col = jnp.sum(jnp.where(square, low[...].astype(F32), 0.0), 1, keepdims=True)
    high_col = jnp.sum(jnp.where(square, high[...].astype(F32), 0.0), 1, keepdims=True)
    rim_lane = iota((rim, mesh_rows), 1).astype(F32)
    low_hot = hot(low_col == rim_lane)
    high_hot = hot(high_col == rim_lane)

    loads[0].wait()
    loads[1].wait()

    def own_term(depth):
        def body(t, c):
            at = pl.ds(pl.multiple_of(t * tile, tile), tile)
            pre[at, :] = mm(edges[at, :], w_edge_in[depth, :latent, :])
            return c

        lax.fori_loop(0, tiles, body, 0)

    def inner_term(depth):
        def body(t, c):
            at = pl.ds(pl.multiple_of(t * tile, tile), tile)
            inner = mm(onehot[at, :prev0], table[depth, :prev0, :])
            if depth == 0:
                pre[at, :] += inner
            else:
                pre[at, :] = inner + mm(edges[at, :], w_edge_in[depth, :latent, :])
            return c

        lax.fori_loop(0, tiles, body, 0)

    own_term(0)

    def arrive_a(k, c):
        from_source(k).wait_recv()
        return c

    others(arrive_a)

    mark = hot(iota((16, width), 1) == channels)
    total[...] = jnp.zeros(total.shape, F32)

    def block(c):
        return recv[pl.ds(c * peers, peers)].reshape(chunk, width)

    for c in range(slots // chunk):
        got = block(c)
        ids = mm_t(mark, got)[0:1, :]
        pick = hot(ids == (iota((mesh_rows, chunk), 0) + 1).astype(F32))
        lat = silu(mm(got, emb_pad[...])).astype(BF16)
        lats[c * chunk : (c + 1) * chunk, :] = lat
        total[...] += mm(pick, lat)
    encoded = total[...].astype(BF16)
    for load in loads[2:4]:
        load.wait()
    state[...] = (
        mesh_feat[...].astype(F32) + rms_norm(mm(encoded, w_g2m[...]), gain_enc[...])
    ).astype(BF16)

    def border_copy(depth, up):
        peer = lax.rem(me + 1, n) if up else lax.rem(me + n - 1, n)
        first = prev0 if up else next0
        return pltpu.make_async_remote_copy(
            src_ref=border.at[depth, int(up)],
            dst_ref=table.at[depth, pl.ds(first, rim)],
            send_sem=h_send.at[depth, int(up)],
            recv_sem=h_recv.at[depth, int(up)],
            device_id={"band": peer},
            device_id_type=MESH_ID,
        )

    for load in loads[4:]:
        load.wait()
    for depth in range(layers):
        own = mm(state[...], w_edge_in[depth, latent : 2 * latent, :]).astype(BF16)
        border[depth, 0] = mm(low_hot, own).astype(BF16)
        border[depth, 1] = mm(high_hot, own).astype(BF16)

        @pl.when(me < n - 1)
        def _():
            border_copy(depth, True).start()

        @pl.when(me > 0)
        def _():
            border_copy(depth, False).start()

        table[depth, own0:prev0, :] = own
        table[depth, :own0, :] = mm(
            state[...], w_edge_in[depth, 2 * latent :, :]
        ).astype(BF16)
        inner_term(depth)
        if depth == 0:
            for c in range(slots // chunk):
                at = slice(c * chunk, (c + 1) * chunk)
                gterm[at, :] = mm(lats[at, :], w_mg[...])
        total[...] = jnp.zeros(total.shape, F32)

        @pl.when(me > 0)
        def _():
            border_copy(depth, True).wait_recv()

        @pl.when(me < n - 1)
        def _():
            border_copy(depth, False).wait_recv()

        def edge_step(t, c):
            at = pl.ds(pl.multiple_of(t * tile, tile), tile)
            hidden = silu(
                pre[at, :] + mm(onehot[at, prev0:], table[depth, prev0:, :])
            ).astype(BF16)
            now = (
                edges[at, :].astype(F32)
                + rms_norm(mm(hidden, w_edge_out[depth]), gain_edge[depth : depth + 1, :])
            ).astype(BF16)
            if depth < layers - 1:
                edges[at, :] = now
            total[...] += mm(rhot[t], now)
            return c

        lax.fori_loop(0, tiles, edge_step, 0)
        summed = total[...].astype(BF16)
        hidden = silu(
            mm(state[...], w_node_in[depth, :latent, :])
            + mm(summed, w_node_in[depth, latent:, :])
        ).astype(BF16)
        state[...] = (
            state[...].astype(F32)
            + rms_norm(mm(hidden, w_node_out[depth]), gain_node[depth : depth + 1, :])
        ).astype(BF16)

    term = mm(state[...], w_mm[...]).astype(BF16)

    def to_source(peer):
        return pltpu.make_async_remote_copy(
            src_ref=reply.at[peer],
            dst_ref=back.at[me],
            send_sem=b_send.at[peer],
            recv_sem=b_recv.at[me],
            device_id={"band": peer},
            device_id_type=MESH_ID,
        )

    def from_owner(peer):
        return pltpu.make_async_remote_copy(
            src_ref=reply.at[me],
            dst_ref=back.at[peer],
            send_sem=b_send.at[me],
            recv_sem=b_recv.at[peer],
            device_id={"band": peer},
            device_id_type=MESH_ID,
        )

    chunks = slots // chunk
    for step in range(chunks):
        c = step
        got = block(c).astype(F32)
        pick = hot(
            got[:, channels : channels + 1] == (iota((chunk, mesh_rows), 1) + 1).astype(F32)
        )
        at = pl.ds(c * chunk, chunk)
        dec = silu(mm(pick, term) + gterm[at, :]).astype(BF16)
        reply[pl.ds(c * peers, peers)] = (
            (got + mm_t(dec, out_pad[...])).astype(BF16).reshape(peers, cap, width)
        )

        def start_b(j, k):
            peer = c * peers + j

            @pl.when(peer != me)
            def _():
                to_source(peer).start()

            return k

        lax.fori_loop(0, peers, start_b, 0)
    back[me] = reply[me]

    def arrive_b(k, c):
        from_owner(partner(k)).wait_recv()
        return c

    others(arrive_b)
    result = jnp.transpose(mm(unpack[...], back[...].reshape(slots, width)))
    out[...] = result.astype(BF16)[:channels, :]

    def sent(k, c):
        to_owner(k).wait_send()
        to_source(partner(k)).wait_send()
        return c

    others(sent)
    for depth in range(layers):

        @pl.when(me < n - 1)
        def _():
            border_copy(depth, True).wait_send()

        @pl.when(me > 0)
        def _():
            border_copy(depth, False).wait_send()


def round_up(value, step):
    return -(-value // step) * step


def shards(
    grid_feats,
    mesh_feat,
    edge_latent,
    g2m_owner,
    g2m_node,
    edge_sender,
    edge_receiver,
    border_low,
    border_high,
    w_embed,
    w_g2m,
    gain_enc,
    w_edge_in,
    w_edge_out,
    gain_edge,
    w_node_in,
    w_node_out,
    gain_node,
    w_m2g_mesh,
    w_m2g_grid,
    w_out,
):
    n = lax.axis_size("band")
    grid_rows, channels = grid_feats.shape
    mesh_rows, latent = mesh_feat.shape
    edge_rows = edge_latent.shape[0]
    layers = w_edge_in.shape[0]
    rim = border_low.shape[1]
    cap = round_up(2 * grid_rows // n, 16)
    slots = n * cap
    chunk = min(slots, 256)
    tile = min(edge_rows, 2048)
    width = round_up(channels + 1, 128)
    table_rows = round_up(2 * mesh_rows + 2 * rim, 128)
    vmem = pl.BlockSpec(memory_space=pltpu.VMEM)
    hbm = pl.BlockSpec(memory_space=pl.ANY)

    def like(a):
        return pltpu.VMEM(a.shape, a.dtype)

    dma = pltpu.SemaphoreType.DMA
    return pl.pallas_call(
        functools.partial(kernel, (n, cap, chunk, tile)),
        out_shape=jax.ShapeDtypeStruct((channels, grid_rows), BF16),
        in_specs=[vmem] * 12 + [hbm] * 9,
        out_specs=vmem,
        scratch_shapes=[
            pltpu.VMEM((width, grid_rows), BF16),
            pltpu.VMEM((width, latent), BF16),
            pltpu.VMEM((width, latent), BF16),
            like(mesh_feat),
            like(edge_latent),
            like(w_g2m),
            like(w_edge_in),
            like(w_edge_out),
            like(w_node_in),
            like(w_node_out),
            like(w_m2g_mesh),
            like(w_m2g_grid),
            pltpu.VMEM((n, cap, width), BF16),
            pltpu.VMEM((n, cap, width), BF16),
            pltpu.VMEM((n, cap, width), BF16),
            pltpu.VMEM((n, cap, width), BF16),
            pltpu.VMEM((grid_rows, slots), BF16),
            pltpu.VMEM((slots, latent), BF16),
            pltpu.VMEM((slots, latent), F32),
            pltpu.VMEM((edge_rows, latent), F32),
            pltpu.VMEM((edge_rows, table_rows), BF16),
            pltpu.VMEM((edge_rows // tile, mesh_rows, tile), BF16),
            pltpu.VMEM((layers, table_rows, latent), BF16),
            pltpu.VMEM((layers, 2, rim, latent), BF16),
            pltpu.VMEM((mesh_rows, latent), F32),
            pltpu.VMEM((mesh_rows, latent), BF16),
            dma((9,)),
            dma((n,)),
            dma((n,)),
            dma((n,)),
            dma((n,)),
            dma((layers, 2)),
            dma((layers, 2)),
        ],
        compiler_params=pltpu.CompilerParams(
            collective_id=0, has_side_effects=True, vmem_limit_bytes=56 * 1024 * 1024
        ),
        cost_estimate=pl.CostEstimate(
            flops=10_000_000_000, bytes_accessed=16_000_000, transcendentals=3_000_000
        ),
    )(
        grid_feats.T,
        g2m_owner.reshape(1, grid_rows),
        g2m_node.reshape(1, grid_rows),
        edge_sender.reshape(edge_rows // 128, 128),
        edge_receiver.reshape(edge_rows // 128, 128),
        border_low,
        border_high,
        gain_enc.reshape(1, latent),
        gain_edge,
        gain_node,
        w_embed,
        w_out.T,
        mesh_feat,
        edge_latent,
        w_g2m,
        w_edge_in,
        w_edge_out,
        w_node_in,
        w_node_out,
        w_m2g_mesh,
        w_m2g_grid,
    ).T


def solution(mesh):
    return jax.shard_map(
        shards,
        mesh=mesh,
        in_specs=(
            P(("groups", "band"), None),
            P("band", None),
            P("band", None),
            P("band", None),
            P("band"),
            P("band"),
            P("band"),
            P("band", None),
            P("band", None),
        )
        + (P(),) * 12,
        out_specs=P(("groups", "band"), None),
        check_vma=False,
    )
```
